256 devices in a mesh: blk: 32 (over x, z), chan: 8 (over y, core).
Axes of the slice: x: 4, y: 4, z: 8, core: 2. Of those that a mesh axis runs over, the one named last changes fastest.
Arguments:
- sky_map: bfloat16 [1792, 128, 2048], P('blk', 'chan'), may hold values from -6 to 6
- cycle_weight: float32 [1792], P('blk'), may hold values from 0.5 to 2
- legendre: bfloat16 [256, 1536, 1792], P('blk', 'chan'), may hold values from -0.125 to 0.125
- kl_filter: bfloat16 [1536, 128, 128], P('chan'), may hold values from -0.5 to 0.5
Outputs:
- filtered_map: bfloat16 [1792, 128, 2048], P('blk', 'chan')
The draws below stay inside these ranges and needn't reach their ends.
All inputs are finite; a program needn't handle non-finite values.
Results may differ from the reference program's by a relative error of at most 0.02.
Values may be sent and summed in bfloat16 or wider, within the bound.
A program may use at most 128 MiB of HBM per device.

```python
import math
import jax
import jax.numpy as jnp
from jax import lax

NPHI = 2048
L = 1536
CH = 128
M = 256
R = 1792


def block_levels(rng, shape, split, least, top_value):
    factor_of = 1.0
    for dim, shards_of in split:
        draws = jax.random.uniform(jax.random.fold_in(jax.random.fold_in(rng, 6), dim), (shards_of,), jnp.float32, least / len(split), top_value / len(split))
        factor_of = factor_of * jnp.repeat(jnp.exp(draws), shape[dim] // shards_of).reshape((-1,) + (1,) * (len(shape) - 1 - dim))
    return factor_of


def noise(key, dims, scale, reach, pieces=(), kind=jnp.bfloat16):
    entries = scale * jax.random.normal(key, dims, jnp.float32)
    if pieces:
        entries = entries * block_levels(key, dims, pieces, -0.22, 0.18)
    return jnp.clip(entries, -reach, reach).astype(kind)


def setup_inputs(seed: int = 0) -> dict:
    splits = jax.random.split(jax.random.key(seed), 5)
    return {
        "sky_map": noise(splits[0], (R, CH, NPHI), 1.0, 6.0, ((0, 32), (1, 8))),
        "cycle_weight": jnp.clip(jnp.exp(math.log(2.0) - 1.3862944 * jax.random.uniform(splits[1], (R,), jnp.float32) ** block_levels(splits[1], (R,), ((0, 32),), -0.2, 0.2)), 0.5, 2.0),
        "legendre": noise(splits[2], (M, L, R), R ** -0.5, 0.125, ((0, 32), (1, 8))),
        "kl_filter": noise(splits[3], (L, CH, CH), CH ** -0.5, 0.5, ((0, 8),)),
    }


def transform_table(pixel_count, mode_count):
    pixel_index = jnp.arange(pixel_count, dtype=jnp.int32)
    mode_index = jnp.arange(mode_count, dtype=jnp.int32)
    phase_index = pixel_index[:, None] * mode_index[None, :] % pixel_count
    angles = phase_index.astype(jnp.float32) * (2.0 * math.pi / pixel_count)
    return jnp.concatenate([jnp.cos(angles), -jnp.sin(angles)], axis=1).astype(jnp.bfloat16)

def reference(sky_map, cycle_weight, legendre, kl_filter):
    cycle_count, chan_count, pixel_count = sky_map.shape
    mode_count, degree_count, cycle_total = legendre.shape
    fourier_table = transform_table(pixel_count, mode_count)
    spectra = jnp.dot(sky_map.reshape(cycle_count * chan_count, pixel_count), fourier_table, preferred_element_type=jnp.float32)
    spectra = spectra.reshape(cycle_count, chan_count, 2 * mode_count) * (cycle_weight[:, None, None] / math.sqrt(pixel_count))
    spectra = spectra.astype(jnp.bfloat16).reshape(cycle_count, chan_count, 2, mode_count)
    by_mode = jnp.moveaxis(spectra, 3, 0)
    kernel = kl_filter.astype(jnp.float32)
    degree_ids = jnp.arange(degree_count, dtype=jnp.int32)

    def one_mode(inputs_mode):
        table_mode, spec_mode, mode_id = inputs_mode
        masked_mode = jnp.where((degree_ids >= mode_id)[:, None], table_mode, jnp.zeros_like(table_mode))
        coeffs = jnp.dot(masked_mode, spec_mode.reshape(cycle_total, chan_count * 2), preferred_element_type=jnp.float32)
        coeffs = coeffs.astype(jnp.bfloat16).reshape(degree_count, chan_count, 2)
        filtered = jnp.einsum('lcd,ldp->lcp', kernel, coeffs.astype(jnp.float32)).astype(jnp.bfloat16)
        synthesis = jnp.dot(masked_mode.T, filtered.reshape(degree_count, chan_count * 2), preferred_element_type=jnp.float32)
        return synthesis.astype(jnp.bfloat16).reshape(cycle_total, chan_count, 2)
    fields = lax.map(one_mode, (legendre, by_mode, jnp.arange(mode_count, dtype=jnp.int32)))
    cycle_field = jnp.transpose(fields, (1, 2, 3, 0)).reshape(cycle_count * chan_count, 2 * mode_count)
    output = jnp.dot(cycle_field, fourier_table.T, preferred_element_type=jnp.float32) / math.sqrt(pixel_count)
    return output.astype(jnp.bfloat16).reshape(cycle_count, chan_count, pixel_count)
```

```python
import functools
import math

import jax
import jax.numpy as jnp
import numpy as np
from jax import lax
from jax.experimental import pallas as pl
from jax.experimental.pallas import tpu as pltpu
from jax.sharding import PartitionSpec as P

F32, BF16 = jnp.float32, jnp.bfloat16
MESH = pl.DeviceIdType.MESH
NT = (((1,), (1,)), ((), ()))
TN = (((0,), (0,)), ((), ()))
NN = (((1,), (0,)), ((), ()))
VMEM_LIMIT = 60 * 2**20
CHUNKS = 4
GX, GZ, GY = 4, 8, 4
NB = GX * GZ


def fourier_table(pixel_count, mode_count):
    phase = np.arange(pixel_count)[:, None] * np.arange(mode_count)[None, :] % pixel_count
    angles = phase.astype(np.float32) * np.float32(2.0 * math.pi / pixel_count)
    table = np.concatenate([np.cos(angles), -np.sin(angles)], axis=1)
    return table.astype(jnp.bfloat16)


def identity(size):
    rows = lax.broadcasted_iota(jnp.int32, (size, size), 0)
    cols = lax.broadcasted_iota(jnp.int32, (size, size), 1)
    return jnp.where(rows == cols, 1.0, 0.0)


def dot(a, b, dims):
    return lax.dot_general(a, b, dims, preferred_element_type=F32)


def forward_kernel(rows, chans, scale, sky_ref, weight_ref, table_ref, out_ref, spec, turned):
    step, steps = pl.program_id(0), pl.num_programs(0)
    block = sky_ref.shape[0]
    x = dot(sky_ref[...], table_ref[...], NN)
    start = pl.multiple_of(step * block, block)
    for t in range(4):
        spec[t, pl.ds(start, block), :] = x[:, 128 * t : 128 * (t + 1)]

    @pl.when(step == steps - 1)
    def _():
        weight = jnp.sum(identity(rows) * weight_ref[...], axis=1, keepdims=True) * scale
        eye = identity(256).astype(BF16)
        pad = jnp.zeros((64 - rows, 256), F32)
        for c in range(chans):
            quarter = [spec[t, pl.ds(c, rows, stride=chans), :] * weight for t in range(4)]
            real = jnp.concatenate(quarter[:2], axis=1)
            imag = jnp.concatenate(quarter[2:], axis=1)
            both = jnp.concatenate([real, pad, imag, pad], axis=0).astype(BF16)
            turned[pl.ds(c, 256, stride=chans), :] = dot(eye, both, NT)
        out_ref[...] = turned[...].astype(BF16)


def forward(sky, weight, table):
    rows, chans, pixels = sky.shape
    steps = 2
    block = rows * chans // steps
    return pl.pallas_call(
        functools.partial(forward_kernel, rows, chans, 1.0 / math.sqrt(pixels)),
        grid=(steps,),
        out_shape=jax.ShapeDtypeStruct((256 * chans, 128), BF16),
        in_specs=[
            pl.BlockSpec((block, pixels), lambda i: (i, 0)),
            pl.BlockSpec((1, rows), lambda i: (0, 0)),
            pl.BlockSpec((pixels, 512), lambda i: (0, 0)),
        ],
        out_specs=pl.BlockSpec((256 * chans, 128), lambda i: (0, 0)),
        scratch_shapes=[
            pltpu.VMEM((4, rows * chans, 128), F32),
            pltpu.VMEM((256 * chans, 128), F32),
        ],
        compiler_params=pltpu.CompilerParams(vmem_limit_bytes=VMEM_LIMIT),
    )(sky.reshape(rows * chans, pixels), weight.reshape(1, rows), table)


def inverse_kernel(rows, chans, scale, field_ref, table_ref, out_ref, wide, lhs):
    step = pl.program_id(0)
    block = out_ref.shape[0]

    @pl.when(step == 0)
    def _():
        wide[...] = field_ref[...].astype(F32)
        eye = identity(128).astype(BF16)
        for c in range(chans):
            here = wide[pl.ds(c, 256, stride=chans), :].astype(BF16)
            turned = dot(eye, here, NT)
            for h in range(2):
                half = turned[:, 128 * h : 128 * (h + 1)]
                lhs[h, pl.ds(c, rows, stride=chans), :] = half[:rows]
                lhs[2 + h, pl.ds(c, rows, stride=chans), :] = half[64 : 64 + rows]

    start = pl.multiple_of(step * block, block)
    left = jnp.concatenate([lhs[t, pl.ds(start, block), :] for t in range(4)], axis=1).astype(BF16)
    for n in range(0, out_ref.shape[1], 512):
        out_ref[:, n : n + 512] = (dot(left, table_ref[:, n : n + 512], NN) * scale).astype(BF16)


def inverse(field, table, rows, chans):
    pixels = table.shape[1]
    steps = 4
    block = rows * chans // steps
    out = pl.pallas_call(
        functools.partial(inverse_kernel, rows, chans, 1.0 / math.sqrt(pixels)),
        grid=(steps,),
        out_shape=jax.ShapeDtypeStruct((rows * chans, pixels), BF16),
        in_specs=[
            pl.BlockSpec((256 * chans, 128), lambda i: (0, 0)),
            pl.BlockSpec((512, pixels), lambda i: (0, 0)),
        ],
        out_specs=pl.BlockSpec((block, pixels), lambda i: (i, 0)),
        scratch_shapes=[
            pltpu.VMEM((256 * chans, 128), F32),
            pltpu.VMEM((4, rows * chans, 128), F32),
        ],
        compiler_params=pltpu.CompilerParams(vmem_limit_bytes=VMEM_LIMIT),
    )(field, table)
    return out.reshape(rows, chans, pixels)


def middle_kernel(
    rows,
    msg_ref,
    leg_hbm,
    kl_hbm,
    out_ref,
    leg,
    kl,
    got,
    spec,
    coef,
    filt,
    part,
    sib_part,
    transit,
    from_up,
    from_dn,
    reply,
    load_sem,
    own_sem,
    a2a_sem,
    ag_send,
    ag_recv,
    rs_send,
    rs_recv,
):
    modes, bands, cycles = leg.shape
    chans = 16
    span = modes // CHUNKS
    per = 2 * span
    b = lax.axis_index("blk")
    k = lax.axis_index("chan")
    y, core = lax.div(k, 2), lax.rem(k, 2)
    y_up, y_dn, y_far = lax.rem(y + 1, GY), lax.rem(y + GY - 1, GY), lax.rem(y + 2, GY)
    up, dn, far, sib = 2 * y_up + core, 2 * y_dn + core, 2 * y_far + core, 2 * y + 1 - core

    load_leg = pltpu.make_async_copy(leg_hbm, leg, load_sem.at[0])
    load_kl = pltpu.make_async_copy(kl_hbm, kl, load_sem.at[1])
    load_leg.start()
    load_kl.start()

    barrier = pltpu.get_barrier_semaphore()
    for other in (up, dn, sib):
        pl.semaphore_signal(barrier, inc=1, device_id={"chan": other}, device_id_type=MESH)

    def greet(j, _):
        pl.semaphore_signal(
            barrier, inc=1, device_id={"blk": lax.rem(b + j, NB)}, device_id_type=MESH
        )
        return 0

    lax.fori_loop(1, NB, greet, 0)
    pl.semaphore_wait(barrier, NB + 2)

    def sel(i):
        return pl.ds(span * i, span)

    def exchange(src, dst, which, i):
        def send(j):
            to = lax.rem(b + j, NB)
            pltpu.make_async_remote_copy(
                src_ref=src.at[to, sel(i)],
                dst_ref=dst.at[b, sel(i)],
                send_sem=a2a_sem.at[which, 0, i],
                recv_sem=a2a_sem.at[which, 1, i],
                device_id={"blk": to},
                device_id_type=MESH,
            ).start()

        def pair(j, _):
            send(j)
            send(NB - j)
            return 0

        lax.fori_loop(1, NB // 2, pair, 0)
        send(NB // 2)
        pltpu.make_async_copy(src.at[b, sel(i)], dst.at[b, sel(i)], own_sem.at[which, i]).start()

    def exchanged(src, dst, which, i):
        return pltpu.make_async_remote_copy(
            src_ref=src.at[pl.ds(0, NB - 1), sel(i)],
            dst_ref=dst.at[pl.ds(0, NB - 1), sel(i)],
            send_sem=a2a_sem.at[which, 0, i],
            recv_sem=a2a_sem.at[which, 1, i],
            device_id={"chan": sib},
            device_id_type=MESH,
        )

    def own_copy(src, dst, which, i):
        return pltpu.make_async_copy(src.at[b, sel(i)], dst.at[b, sel(i)], own_sem.at[which, i])

    def copy(src, dst, send, recv, slot, i, to):
        return pltpu.make_async_remote_copy(
            src_ref=src,
            dst_ref=dst,
            send_sem=send.at[i, slot],
            recv_sem=recv.at[i, slot],
            device_id={"chan": to},
            device_id_type=MESH,
        )

    def shard(i, owner, parts=None):
        lanes = pl.ds(pl.multiple_of(chans * owner, chans), chans)
        if parts is None:
            return spec.at[sel(i), :, lanes, :]
        return spec.at[sel(i), pl.ds(parts, 1), lanes, :]

    def gather_copy(slot, i):
        src, to = (
            (shard(i, k), up),
            (shard(i, k), dn),
            (shard(i, k), sib),
            (shard(i, dn, 0), up),
            (shard(i, up, 1), dn),
            (shard(i, dn), sib),
            (shard(i, up), sib),
            (shard(i, far, 0), sib),
            (shard(i, far, 1), sib),
        )[slot]
        return copy(src, src, ag_send, ag_recv, slot, i, to)

    def scatter_copy(slot, i):
        src, dst, to = (
            (part.at[sel(i), 1 - core], sib_part.at[sel(i)], sib),
            (part.at[sel(i), core, 0, y_far], transit.at[0, sel(i)], up),
            (part.at[sel(i), core, 1, y_far], transit.at[1, sel(i)], dn),
            (part.at[sel(i), core, 1, y_up], from_dn.at[1, sel(i)], up),
            (part.at[sel(i), core, 0, y_dn], from_up.at[0, sel(i)], dn),
            (transit.at[0, sel(i)], from_dn.at[0, sel(i)], up),
            (transit.at[1, sel(i)], from_up.at[1, sel(i)], dn),
        )[slot]
        return copy(src, dst, rs_send, rs_recv, slot, i, to)

    for i in range(CHUNKS):
        exchange(msg_ref, got, 0, i)

    def assemble(i):
        exchanged(msg_ref, got, 0, i).wait_recv()
        own_copy(msg_ref, got, 0, i).wait()
        mine = pl.ds(pl.multiple_of(chans * k, chans), chans)
        for m in range(span * i, span * (i + 1)):
            for p in range(2):
                pieces = [got[s, m, :, 64 * p : 64 * p + rows] for s in range(NB)]
                spec[m, p, mine, :] = jnp.concatenate(pieces, axis=1)
        for slot in (0, 1, 2):
            gather_copy(slot, i).start()

    def pass_on(i):
        gather_copy(0, i).wait_recv()
        gather_copy(3, i).start()
        gather_copy(5, i).start()
        gather_copy(1, i).wait_recv()
        gather_copy(4, i).start()
        gather_copy(6, i).start()

    def pass_far(i):
        gather_copy(3, i).wait_recv()
        gather_copy(7, i).start()
        gather_copy(4, i).wait_recv()
        gather_copy(8, i).start()

    def legendre(i):
        for slot in (2, 5, 6, 7, 8):
            gather_copy(slot, i).wait_recv()
        if i == 0:
            load_leg.wait()
            load_kl.wait()
        degree = k * bands + lax.broadcasted_iota(jnp.int32, (bands, 128), 0)
        for n in range(span):
            m = span * i + n
            sums = dot(leg[m], spec[m].reshape(2 * 128, cycles), NT)
            for p in range(2):
                kept = jnp.where(degree >= b * modes + m, sums[:, 128 * p : 128 * (p + 1)], 0.0)
                coef[pl.ds(2 * n + p, bands, stride=per), :] = kept

        group = 16 // per
        row_group = lax.div(lax.broadcasted_iota(jnp.int32, (16, 128), 0), per)

        def channels(g, _):
            for u in range(4):
                at = pl.multiple_of(16 * (4 * g + u), 16)
                left = coef[pl.ds(at, 16), :].astype(BF16)
                table = kl[pl.ds(group * (4 * g + u), group)]
                mixed = dot(left, table.reshape(group * 128, 128), NT)
                picked = mixed[:, :128]
                for t in range(1, group):
                    picked = jnp.where(row_group == t, mixed[:, 128 * t : 128 * (t + 1)], picked)
                filt[pl.ds(at, 16), :] = picked
            return 0

        lax.fori_loop(0, bands // group // 4, channels, 0)
        for n in range(span):
            m = span * i + n
            sides = [filt[pl.ds(2 * n + p, bands, stride=per), :].astype(BF16) for p in range(2)]
            left = jnp.concatenate(sides, axis=1).T
            for at in range(0, cycles, 256):
                tile = dot(left, leg[m, :, at : at + 256], NN).astype(BF16)
                for p in range(2):
                    for o in range(8):
                        first = 128 * p + 16 * o
                        part[m, o % 2, p, o // 2, :, at : at + 256] = tile[first : first + 16]
        scatter_copy(0, i).start()

    def add_sibling(i):
        scatter_copy(0, i).wait_recv()

        def add(t, _):
            m, p = span * i + lax.div(t, 2), lax.rem(t, 2)
            total = part[m, core, p].astype(F32) + sib_part[m, p].astype(F32)
            part[m, core, p] = total.astype(BF16)
            return 0

        lax.fori_loop(0, per, add, 0)
        for slot in (1, 2, 3, 4):
            scatter_copy(slot, i).start()

    def add_transit(i):
        for way, nearer in ((0, y_up), (1, y_dn)):
            scatter_copy(1 + way, i).wait_recv()
            for m in range(span * i, span * (i + 1)):
                total = transit[way, m].astype(F32) + part[m, core, way, nearer].astype(F32)
                transit[way, m] = total.astype(BF16)
            scatter_copy(5 + way, i).start()

    def answer(i):
        for slot in (3, 4, 5, 6):
            scatter_copy(slot, i).wait_recv()
        zeros = jnp.zeros((16, 64 - rows), F32)
        for m in range(span * i, span * (i + 1)):
            both = [
                part[m, core, p, y].astype(F32)
                + from_up[p, m].astype(F32)
                + from_dn[p, m].astype(F32)
                for p in range(2)
            ]
            for s in range(NB):
                lanes = slice(rows * s, rows * (s + 1))
                line = jnp.concatenate([both[0][:, lanes], zeros, both[1][:, lanes], zeros], axis=1)
                reply[s, m] = line.astype(BF16)
        exchange(reply, out_ref, 1, i)

    stages = (assemble, pass_on, pass_far, legendre, add_sibling, add_transit, answer)
    for tick in range(CHUNKS + len(stages) - 1):
        for n in reversed(range(len(stages))):
            if 0 <= tick - n < CHUNKS:
                stages[n](tick - n)

    for i in range(CHUNKS):
        last = exchanged(reply, out_ref, 1, i)
        last.wait_recv()
        own_copy(reply, out_ref, 1, i).wait()
        exchanged(msg_ref, got, 0, i).wait_send()
        last.wait_send()
        for slot in range(9):
            gather_copy(slot, i).wait_send()
        for slot in range(7):
            scatter_copy(slot, i).wait_send()


def middle(messages, legendre, kl, rows):
    modes, bands, cycles = legendre.shape
    chans = messages.shape[2]
    per = 2 * modes // CHUNKS
    vmem = pl.BlockSpec(memory_space=pltpu.VMEM)
    hbm = pl.BlockSpec(memory_space=pl.ANY)
    dma = pltpu.SemaphoreType.DMA
    return pl.pallas_call(
        functools.partial(middle_kernel, rows),
        out_shape=jax.ShapeDtypeStruct(messages.shape, BF16),
        in_specs=[vmem, hbm, hbm],
        out_specs=vmem,
        scratch_shapes=[
            pltpu.VMEM(legendre.shape, BF16),
            pltpu.VMEM(kl.shape, BF16),
            pltpu.VMEM(messages.shape, BF16),
            pltpu.VMEM((modes, 2, 128, cycles), BF16),
            pltpu.VMEM((bands * per, 128), F32),
            pltpu.VMEM((bands * per, 128), F32),
            pltpu.VMEM((modes, 2, 2, GY, chans, cycles), BF16),
            pltpu.VMEM((modes, 2, GY, chans, cycles), BF16),
            pltpu.VMEM((2, modes, chans, cycles), BF16),
            pltpu.VMEM((2, modes, chans, cycles), BF16),
            pltpu.VMEM((2, modes, chans, cycles), BF16),
            pltpu.VMEM(messages.shape, BF16),
            dma((2,)),
            dma((2, CHUNKS)),
            dma((2, 2, CHUNKS)),
            dma((CHUNKS, 9)),
            dma((CHUNKS, 9)),
            dma((CHUNKS, 7)),
            dma((CHUNKS, 7)),
        ],
        compiler_params=pltpu.CompilerParams(
            collective_id=0, has_side_effects=True, vmem_limit_bytes=VMEM_LIMIT
        ),
        cost_estimate=pl.CostEstimate(
            flops=6 * 10**9, bytes_accessed=14 * 10**6, transcendentals=0
        ),
    )(messages, legendre, kl)


def shards(sky_map, cycle_weight, legendre, kl_filter):
    rows, chans, pixels = sky_map.shape
    modes = legendre.shape[0]
    table = fourier_table(pixels, modes * NB)
    messages = forward(sky_map, cycle_weight, jnp.asarray(table))
    field = middle(messages.reshape(NB, modes, chans, 128), legendre, kl_filter, rows)
    return inverse(field.reshape(NB * modes * chans, 128), jnp.asarray(table.T.copy()), rows, chans)


def solution(mesh):
    in_specs = (P("blk", "chan", None), P("blk"), P("blk", "chan", None), P("chan", None, None))
    out_specs = P("blk", "chan", None)
    return jax.shard_map(shards, mesh=mesh, in_specs=in_specs, out_specs=out_specs, check_vma=False)
```

```python
import functools
import math

import jax
import jax.numpy as jnp
import numpy as np
from jax import lax
from jax.experimental import pallas as pl
from jax.experimental.pallas import tpu as pltpu
from jax.sharding import PartitionSpec as P

F32, BF16 = jnp.float32, jnp.bfloat16
MESH = pl.DeviceIdType.MESH
NT = (((1,), (1,)), ((), ()))
NN = (((1,), (0,)), ((), ()))
VMEM_LIMIT = 60 * 2**20
GX, GZ, GY = 4, 8, 4
NB = GX * GZ
MODES, GROUP = 8, 2
UNROLL = 4
AHEAD = 4
SCATTER, WINDOW, LAG = 3, 1, 2


def fourier_table(pixel_count, mode_count):
    phase = np.arange(pixel_count)[:, None] * np.arange(mode_count)[None, :] % pixel_count
    angles = phase.astype(np.float32) * np.float32(2.0 * math.pi / pixel_count)
    both = np.stack([np.cos(angles), -np.sin(angles)], axis=1).astype(jnp.bfloat16)
    both = both.reshape(pixel_count, 2, NB, 2, MODES // 2)
    return both.transpose(0, 3, 1, 4, 2).reshape(pixel_count, 2 * mode_count)


def identity(size):
    rows = lax.broadcasted_iota(jnp.int32, (size, size), 0)
    cols = lax.broadcasted_iota(jnp.int32, (size, size), 1)
    return jnp.where(rows == cols, 1.0, 0.0)


def dot(a, b, dims):
    return lax.dot_general(a, b, dims, preferred_element_type=F32)


def plan():
    steps = [("transform", 0), ("transform", 1), ("assemble", 0), ("assemble", 1), ("pass_on", 0)]
    for t in range(MODES + SCATTER + 4):
        steps += [("assemble", t + 2), ("pass_on", t + 1), ("pass_far", t)]
        r = t - SCATTER
        steps += [("add_transit", r - 1)]
        steps += [("add_sibling", i) for i in range(WINDOW - 1) if r == 0]
        steps += [("add_sibling", r + WINDOW - 1 if r >= 0 else -1), ("answer", r - LAG)]
        if t % 2:
            steps += [("analyse", (t - 1) // 2)]
        else:
            steps += [("synthesise", (t - 2) // 2)]
    steps += [("finish", 0), ("finish", 1)]
    count = {"transform": 2, "finish": 2, "analyse": MODES // GROUP, "synthesise": MODES // GROUP}
    return [(name, i) for name, i in steps if 0 <= i < count.get(name, MODES)]


def main_kernel(
    sky_hbm,
    weight_ref,
    table_hbm,
    leg_hbm,
    kl_hbm,
    out_ref,
    sky,
    table,
    leg,
    kl,
    wave,
    wide,
    msg,
    got,
    spec,
    coef,
    filt,
    part,
    sib_part,
    transit,
    from_up,
    from_dn,
    reply,
    back,
    load_sem,
    own_sem,
    a2a_sem,
    ag_send,
    ag_recv,
    rs_send,
    rs_recv,
):
    modes, bands, cycles = leg.shape
    chans, pixels = 16, sky.shape[1]
    rows = sky.shape[0] // chans
    half = modes // 2
    per = 2 * GROUP
    b = lax.axis_index("blk")
    k = lax.axis_index("chan")
    y, core = lax.div(k, 2), lax.rem(k, 2)
    y_up, y_dn, y_far = lax.rem(y + 1, GY), lax.rem(y + GY - 1, GY), lax.rem(y + 2, GY)
    up, dn, far, sib = 2 * y_up + core, 2 * y_dn + core, 2 * y_far + core, 2 * y + 1 - core

    load_sky = pltpu.make_async_copy(sky_hbm, sky, load_sem.at[0])
    load_table = pltpu.make_async_copy(table_hbm, table, load_sem.at[1])
    load_leg = pltpu.make_async_copy(leg_hbm, leg, load_sem.at[2])
    load_kl = pltpu.make_async_copy(kl_hbm, kl, load_sem.at[3])
    load_sky.start()
    load_table.start()

    barrier = pltpu.get_barrier_semaphore()
    for other in (up, dn, sib):
        pl.semaphore_signal(barrier, inc=1, device_id={"chan": other}, device_id_type=MESH)

    def greet(j, _):
        pl.semaphore_signal(
            barrier, inc=1, device_id={"blk": lax.rem(b + j, NB)}, device_id_type=MESH
        )
        return 0

    lax.fori_loop(1, NB, greet, 0)

    def own_copy(src, dst, which, i):
        return pltpu.make_async_copy(src.at[i, b], dst.at[i, b], own_sem.at[which, i])

    def exchange(src, dst, which, i):
        def send(j):
            to = lax.rem(b + j, NB)
            pltpu.make_async_remote_copy(
                src_ref=src.at[i, to],
                dst_ref=dst.at[i, b],
                send_sem=a2a_sem.at[which, 0, i],
                recv_sem=a2a_sem.at[which, 1, i],
                device_id={"blk": to},
                device_id_type=MESH,
            ).start()

        def pair(j, _):
            send(j)
            send(NB - j)
            return 0

        lax.fori_loop(1, NB // 2, pair, 0)
        send(NB // 2)
        own_copy(src, dst, which, i).start()

    def exchanged(src, dst, which, i):
        return pltpu.make_async_remote_copy(
            src_ref=src.at[i, pl.ds(0, NB - 1)],
            dst_ref=dst.at[i, pl.ds(0, NB - 1)],
            send_sem=a2a_sem.at[which, 0, i],
            recv_sem=a2a_sem.at[which, 1, i],
            device_id={"chan": sib},
            device_id_type=MESH,
        )

    def copy(src, dst, send, recv, slot, i, to):
        return pltpu.make_async_remote_copy(
            src_ref=src,
            dst_ref=dst,
            send_sem=send.at[i, slot],
            recv_sem=recv.at[i, slot],
            device_id={"chan": to},
            device_id_type=MESH,
        )

    def shard(i, owner, p=None):
        at = pl.ds(pl.multiple_of(chans * owner, chans), chans)
        return spec.at[i, :, at, :] if p is None else spec.at[i, p, at, :]

    def gather_copy(slot, i):
        src, to = (
            (shard(i, k), up),
            (shard(i, k), dn),
            (shard(i, k), sib),
            (shard(i, dn, 0), up),
            (shard(i, up, 1), dn),
            (shard(i, dn), sib),
            (shard(i, up), sib),
            (shard(i, far, 0), sib),
            (shard(i, far, 1), sib),
        )[slot]
        return copy(src, src, ag_send, ag_recv, slot, i, to)

    def scatter_copy(slot, i):
        src, dst, to = (
            (part.at[i, 1 - core], sib_part.at[i], sib),
            (part.at[i, core, 0, y_far], transit.at[0, i], up),
            (part.at[i, core, 1, y_far], transit.at[1, i], dn),
            (part.at[i, core, 1, y_up], from_dn.at[1, i], up),
            (part.at[i, core, 0, y_dn], from_up.at[0, i], dn),
            (transit.at[0, i], from_dn.at[0, i], up),
            (transit.at[1, i], from_up.at[1, i], dn),
        )[slot]
        return copy(src, dst, rs_send, rs_recv, slot, i, to)

    def transform(h):
        if h == 0:
            load_sky.wait()
            load_table.wait()
            load_leg.start()
            load_kl.start()
        weight = jnp.sum(identity(rows) * weight_ref[...], axis=1, keepdims=True)
        weight = weight * (1.0 / math.sqrt(pixels))
        eye = identity(128).astype(BF16)
        pad = jnp.zeros((64 - rows, 128), F32)
        found = dot(sky[...], table[:, 256 * h : 256 * (h + 1)], NN)
        for p in range(2):
            wave[p] = found[:, 128 * p : 128 * (p + 1)]
        for c in range(chans):
            real, imag = (wave[p, pl.ds(c, rows, stride=chans), :] * weight for p in range(2))
            both = jnp.concatenate([real, pad, imag, pad], axis=0).astype(BF16)
            wide[pl.ds(c, 128, stride=chans), :] = dot(eye, both, NT)
        for i in range(half):
            turned = wide[NB * chans * i : NB * chans * (i + 1), :].astype(BF16)
            msg[half * h + i] = turned.reshape(NB, chans, 128)
        if h == 0:
            pl.semaphore_wait(barrier, NB + 2)
            for i in range(AHEAD):
                exchange(msg, got, 0, i)

    def assemble(i):
        exchanged(msg, got, 0, i).wait_recv()
        own_copy(msg, got, 0, i).wait()
        if i + AHEAD < modes:
            exchange(msg, got, 0, i + AHEAD)
        mine = pl.ds(pl.multiple_of(chans * k, chans), chans)
        for p in range(2):
            pieces = [got[i, s, :, 64 * p : 64 * p + rows] for s in range(NB)]
            spec[i, p, mine, :] = jnp.concatenate(pieces, axis=1)
        for slot in range(3):
            gather_copy(slot, i).start()

    def pass_on(i):
        for n in range(2):
            gather_copy(n, i).wait_recv()
            gather_copy(3 + n, i).start()
            gather_copy(5 + n, i).start()

    def pass_far(i):
        for n in range(2):
            gather_copy(3 + n, i).wait_recv()
            gather_copy(7 + n, i).start()

    each = 16 // per
    rounds = bands // each // UNROLL

    def channels(g, _):
        row_group = lax.div(lax.broadcasted_iota(jnp.int32, (16, 128), 0), per)
        for u in range(UNROLL):
            at = pl.multiple_of(16 * (UNROLL * g + u), 16)
            left = coef[pl.ds(at, 16), :].astype(BF16)
            square = kl[pl.ds(each * (UNROLL * g + u), each)]
            mixed = dot(left, square.reshape(each * 128, 128), NT)
            picked = mixed[:, :128]
            for t in range(1, each):
                picked = jnp.where(row_group == t, mixed[:, 128 * t : 128 * (t + 1)], picked)
            filt[pl.ds(at, 16), :] = picked
        return 0

    def analyse(g):
        if g == 0:
            load_leg.wait()
            load_kl.wait()
        degree = k * bands + lax.broadcasted_iota(jnp.int32, (bands, 128), 0)
        for n in range(GROUP):
            i = GROUP * g + n
            for slot in (2, 5, 6, 7, 8):
                gather_copy(slot, i).wait_recv()
            sums = dot(leg[i], spec[i].reshape(2 * 128, cycles), NT)
            for p in range(2):
                kept = jnp.where(degree >= b * modes + i, sums[:, 128 * p : 128 * (p + 1)], 0.0)
                coef[pl.ds(2 * n + p, bands, stride=per), :] = kept
        lax.fori_loop(0, rounds // 2, channels, 0)

    def synthesise(g):
        lax.fori_loop(rounds // 2, rounds, channels, 0)
        for n in range(GROUP):
            i = GROUP * g + n
            sides = [filt[pl.ds(2 * n + p, bands, stride=per), :].astype(BF16) for p in range(2)]
            left = jnp.concatenate(sides, axis=1).T
            for at in range(0, cycles, 256):
                tile = dot(left, leg[i, :, at : at + 256], NN).astype(BF16)
                for p in range(2):
                    for o in range(8):
                        first = 128 * p + 16 * o
                        part[i, o % 2, p, o // 2, :, at : at + 256] = tile[first : first + 16]
            scatter_copy(0, i).start()

    def add_sibling(i):
        scatter_copy(0, i).wait_recv()

        def add(p, _):
            total = part[i, core, p].astype(F32) + sib_part[i, p].astype(F32)
            part[i, core, p] = total.astype(BF16)
            return 0

        lax.fori_loop(0, 2, add, 0)
        for slot in (1, 2, 3, 4):
            scatter_copy(slot, i).start()

    def add_transit(i):
        for n, nearer in ((0, y_up), (1, y_dn)):
            scatter_copy(1 + n, i).wait_recv()
            total = transit[n, i].astype(F32) + part[i, core, n, nearer].astype(F32)
            transit[n, i] = total.astype(BF16)
            scatter_copy(5 + n, i).start()

    def answer(i):
        for slot in (3, 4, 5, 6):
            scatter_copy(slot, i).wait_recv()
        zeros = jnp.zeros((16, 64 - rows), F32)
        both = [
            part[i, core, p, y].astype(F32)
            + from_up[p, i].astype(F32)
            + from_dn[p, i].astype(F32)
            for p in range(2)
        ]
        for s in range(NB):
            lanes = slice(rows * s, rows * (s + 1))
            line = jnp.concatenate([both[0][:, lanes], zeros, both[1][:, lanes], zeros], axis=1)
            reply[i, s] = line.astype(BF16)
        exchange(reply, back, 1, i)

    def finish(h):
        eye = identity(128).astype(BF16)
        for i in range(half):
            exchanged(reply, back, 1, half * h + i).wait_recv()
            own_copy(reply, back, 1, half * h + i).wait()
            turned = back[half * h + i].reshape(NB * chans, 128)
            wide[NB * chans * i : NB * chans * (i + 1), :] = turned.astype(F32)
        for c in range(chans):
            here = wide[pl.ds(c, 128, stride=chans), :].astype(BF16)
            turned = dot(eye, here, NT)
            for p in range(2):
                wave[p, pl.ds(c, rows, stride=chans), :] = turned[64 * p : 64 * p + rows]
        for p in range(2):
            at = 256 * h + 128 * p
            out_ref[:, at : at + 128] = wave[p].astype(BF16)

    stages = {
        f.__name__: f
        for f in (
            transform,
            assemble,
            pass_on,
            pass_far,
            analyse,
            synthesise,
            add_sibling,
            add_transit,
            answer,
            finish,
        )
    }
    for name, i in plan():
        stages[name](i)

    for i in range(modes):
        exchanged(msg, got, 0, i).wait_send()
        exchanged(reply, back, 1, i).wait_send()
        for slot in range(9):
            gather_copy(slot, i).wait_send()
        for slot in range(7):
            scatter_copy(slot, i).wait_send()


def main_call(sky, weight, table, legendre, kl):
    modes, bands, cycles = legendre.shape
    chans, (lines, pixels) = 16, sky.shape
    per = 2 * GROUP
    vmem = pl.BlockSpec(memory_space=pltpu.VMEM)
    hbm = pl.BlockSpec(memory_space=pl.ANY)
    dma = pltpu.SemaphoreType.DMA
    messages = pltpu.VMEM((modes, NB, chans, 128), BF16)
    return pl.pallas_call(
        main_kernel,
        out_shape=jax.ShapeDtypeStruct((lines, 512), BF16),
        in_specs=[hbm, vmem, hbm, hbm, hbm],
        out_specs=vmem,
        scratch_shapes=[
            pltpu.VMEM(sky.shape, BF16),
            pltpu.VMEM(table.shape, BF16),
            pltpu.VMEM(legendre.shape, BF16),
            pltpu.VMEM(kl.shape, BF16),
            pltpu.VMEM((2, lines, 128), F32),
            pltpu.VMEM((modes // 2 * NB * chans, 128), F32),
            messages,
            messages,
            pltpu.VMEM((modes, 2, 128, cycles), BF16),
            pltpu.VMEM((bands * per, 128), F32),
            pltpu.VMEM((bands * per, 128), F32),
            pltpu.VMEM((modes, 2, 2, GY, chans, cycles), BF16),
            pltpu.VMEM((modes, 2, GY, chans, cycles), BF16),
            pltpu.VMEM((2, modes, chans, cycles), BF16),
            pltpu.VMEM((2, modes, chans, cycles), BF16),
            pltpu.VMEM((2, modes, chans, cycles), BF16),
            messages,
            messages,
            dma((4,)),
            dma((2, modes)),
            dma((2, 2, modes)),
            dma((modes, 9)),
            dma((modes, 9)),
            dma((modes, 7)),
            dma((modes, 7)),
        ],
        compiler_params=pltpu.CompilerParams(
            collective_id=0, has_side_effects=True, vmem_limit_bytes=VMEM_LIMIT
        ),
        cost_estimate=pl.CostEstimate(
            flops=8 * 10**9, bytes_accessed=18 * 10**6, transcendentals=0
        ),
    )(sky, weight, table, legendre, kl)


def inverse_kernel(scale, field_ref, table_ref, out_ref):
    out_ref[...] = (dot(field_ref[...], table_ref[...], NN) * scale).astype(BF16)


def inverse(field, table):
    lines, pixels = field.shape[0], table.shape[1]
    block = 512
    return pl.pallas_call(
        functools.partial(inverse_kernel, 1.0 / math.sqrt(pixels)),
        grid=(pixels // block,),
        out_shape=jax.ShapeDtypeStruct((lines, pixels), BF16),
        in_specs=[
            pl.BlockSpec(field.shape, lambda i: (0, 0)),
            pl.BlockSpec((512, block), lambda i: (0, i)),
        ],
        out_specs=pl.BlockSpec((lines, block), lambda i: (0, i)),
        compiler_params=pltpu.CompilerParams(vmem_limit_bytes=VMEM_LIMIT),
    )(field, table)


def shards(sky_map, cycle_weight, legendre, kl_filter):
    rows, chans, pixels = sky_map.shape
    table = fourier_table(pixels, legendre.shape[0] * NB)
    sky = sky_map.reshape(rows * chans, pixels)
    weight = cycle_weight.reshape(1, rows)
    field = main_call(sky, weight, jnp.asarray(table), legendre, kl_filter)
    return inverse(field, jnp.asarray(table.T.copy())).reshape(rows, chans, pixels)


def solution(mesh):
    in_specs = (P("blk", "chan", None), P("blk"), P("blk", "chan", None), P("chan", None, None))
    out_specs = P("blk", "chan", None)
    return jax.shard_map(shards, mesh=mesh, in_specs=in_specs, out_specs=out_specs, check_vma=False)
```

```python
import functools
import math

import jax
import jax.numpy as jnp
import numpy as np
from jax import lax
from jax.experimental import pallas as pl
from jax.experimental.pallas import tpu as pltpu
from jax.sharding import PartitionSpec as P

F32, BF16 = jnp.float32, jnp.bfloat16
MESH = pl.DeviceIdType.MESH
NT = (((1,), (1,)), ((), ()))
NN = (((1,), (0,)), ((), ()))
VMEM_LIMIT = 60 * 2**20
GX, GZ, GY = 4, 8, 4
NB = GX * GZ
MODES, GROUP = 8, 2
UNROLL = 12
BLOCK = 1024
AHEAD = 3
SCATTER, WINDOW, LAG = 3, 1, 2
ORDER = (0, 1, 2, 4, 5, 6, 7, 3)
EARLY = ORDER[-1]


def fourier_table(pixel_count, mode_count):
    phase = np.arange(pixel_count)[:, None] * np.arange(mode_count)[None, :] % pixel_count
    angles = phase.astype(np.float32) * np.float32(2.0 * math.pi / pixel_count)
    both = np.stack([np.cos(angles), -np.sin(angles)], axis=1).astype(jnp.bfloat16)
    both = both.reshape(pixel_count, 2, NB, 2, MODES // 2)
    return both.transpose(0, 3, 1, 4, 2).reshape(pixel_count, 2 * mode_count)


def identity(size):
    rows = lax.broadcasted_iota(jnp.int32, (size, size), 0)
    cols = lax.broadcasted_iota(jnp.int32, (size, size), 1)
    return jnp.where(rows == cols, 1.0, 0.0)


def dot(a, b, dims):
    return lax.dot_general(a, b, dims, preferred_element_type=F32)


def plan():
    steps = [("transform", 0), ("early_send", 0), ("transform", 1), ("early_pass", 0)]
    steps += [("assemble", 0), ("assemble", 1), ("pass_on", 0)]
    for t in range(MODES + SCATTER + 4):
        steps += [("early_exchange", t - 3)]
        steps += [("assemble", t + 2 if t + 2 < MODES - 1 else -1)]
        steps += [("pass_on", t + 1), ("pass_far", t)]
        r = t - SCATTER
        steps += [("add_transit", r - 1)]
        steps += [("add_sibling", i) for i in range(WINDOW - 1) if r == 0]
        steps += [("add_sibling", r + WINDOW - 1 if r >= 0 else -1), ("answer", r - LAG)]
        steps += [("assemble", MODES - 1 if t == MODES - 1 else -1)]
        if t % 2:
            steps += [("analyse", (t - 1) // 2)]
        else:
            steps += [("synthesise", (t - 2) // 2)]
    steps += [("finish", 1), ("finish", 0)]
    count = {"transform": 2, "finish": 2, "analyse": MODES // GROUP, "synthesise": MODES // GROUP}
    count |= {"early_send": 1, "early_pass": 1, "early_exchange": 1}
    return [(name, i) for name, i in steps if 0 <= i < count.get(name, MODES)]


def main_kernel(
    sky_hbm,
    weight_ref,
    table_hbm,
    leg_hbm,
    kl_hbm,
    out_ref,
    sky,
    table,
    leg,
    kl,
    wave,
    wide,
    msg,
    got,
    early,
    late,
    spec,
    coef,
    filt,
    part,
    sib_part,
    transit,
    from_up,
    from_dn,
    reply,
    back,
    load_sem,
    own_sem,
    a2a_sem,
    ag_send,
    ag_recv,
    rs_send,
    rs_recv,
):
    modes, bands, cycles = leg.shape
    chans, pixels = 16, sky.shape[1]
    rows = sky.shape[0] // chans
    half = modes // 2
    per = 2 * GROUP
    b = lax.axis_index("blk")
    k = lax.axis_index("chan")
    y, core = lax.div(k, 2), lax.rem(k, 2)
    y_up, y_dn, y_far = lax.rem(y + 1, GY), lax.rem(y + GY - 1, GY), lax.rem(y + 2, GY)
    up, dn, far, sib = 2 * y_up + core, 2 * y_dn + core, 2 * y_far + core, 2 * y + 1 - core

    load_sky = pltpu.make_async_copy(sky_hbm, sky, load_sem.at[0])
    load_table = pltpu.make_async_copy(table_hbm, table, load_sem.at[1])
    load_leg = pltpu.make_async_copy(leg_hbm, leg, load_sem.at[2])
    load_kl = pltpu.make_async_copy(kl_hbm, kl, load_sem.at[3])
    load_sky.start()
    load_table.start()

    barrier = pltpu.get_barrier_semaphore()
    for other in (up, dn, sib):
        pl.semaphore_signal(barrier, inc=1, device_id={"chan": other}, device_id_type=MESH)

    def greet(j, _):
        pl.semaphore_signal(
            barrier, inc=1, device_id={"blk": lax.rem(b + j, NB)}, device_id_type=MESH
        )
        return 0

    lax.fori_loop(1, NB, greet, 0)

    def own_copy(src, dst, which, i):
        if which == 0 and i == EARLY:
            return pltpu.make_async_copy(early.at[:, b], late.at[b], own_sem.at[which, i])
        return pltpu.make_async_copy(src.at[i, b], dst.at[i, b], own_sem.at[which, i])

    def exchange(src, dst, which, i):
        def send(j):
            to = lax.rem(b + j, NB)
            first = which == 0 and i == EARLY
            pltpu.make_async_remote_copy(
                src_ref=early.at[:, to] if first else src.at[i, to],
                dst_ref=late.at[b] if first else dst.at[i, b],
                send_sem=a2a_sem.at[which, 0, i],
                recv_sem=a2a_sem.at[which, 1, i],
                device_id={"blk": to},
                device_id_type=MESH,
            ).start()

        def pair(j, _):
            send(j)
            send(NB - j)
            return 0

        lax.fori_loop(1, NB // 2, pair, 0)
        send(NB // 2)
        own_copy(src, dst, which, i).start()

    def exchanged(src, dst, which, i):
        some = pl.ds(0, NB - 1)
        first = which == 0 and i == EARLY
        return pltpu.make_async_remote_copy(
            src_ref=late.at[some] if first else src.at[i, some],
            dst_ref=late.at[some] if first else dst.at[i, some],
            send_sem=a2a_sem.at[which, 0, i],
            recv_sem=a2a_sem.at[which, 1, i],
            device_id={"chan": sib},
            device_id_type=MESH,
        )

    def copy(src, dst, send, recv, slot, i, to):
        return pltpu.make_async_remote_copy(
            src_ref=src,
            dst_ref=dst,
            send_sem=send.at[i, slot],
            recv_sem=recv.at[i, slot],
            device_id={"chan": to},
            device_id_type=MESH,
        )

    def shard(i, owner, p=None):
        at = pl.ds(pl.multiple_of(chans * owner, chans), chans)
        return spec.at[i, :, at, :] if p is None else spec.at[i, p, at, :]

    def gather_copy(slot, i):
        src, to = (
            (shard(i, k), up),
            (shard(i, k), dn),
            (shard(i, k), sib),
            (shard(i, dn, 0), up),
            (shard(i, up, 1), dn),
            (shard(i, dn), sib),
            (shard(i, up), sib),
            (shard(i, far, 0), sib),
            (shard(i, far, 1), sib),
        )[slot]
        if i == EARLY and slot in (0, 1, 3, 4):
            src = (
                early.at[y],
                early.at[y],
                None,
                early.at[y_dn, pl.ds(0, NB // 2)],
                early.at[y_up, pl.ds(NB // 2, NB // 2)],
            )[slot]
        return copy(src, src, ag_send, ag_recv, slot, i, to)

    def scatter_copy(slot, i):
        src, dst, to = (
            (part.at[i, 1 - core], sib_part.at[i], sib),
            (part.at[i, core, 0, y_far], transit.at[0, i], up),
            (part.at[i, core, 1, y_far], transit.at[1, i], dn),
            (part.at[i, core, 1, y_up], from_dn.at[1, i], up),
            (part.at[i, core, 0, y_dn], from_up.at[0, i], dn),
            (transit.at[0, i], from_dn.at[0, i], up),
            (transit.at[1, i], from_up.at[1, i], dn),
        )[slot]
        return copy(src, dst, rs_send, rs_recv, slot, i, to)

    def transform(h):
        if h == 0:
            load_sky.wait()
            load_table.wait()
            load_leg.start()
            load_kl.start()
        weight = jnp.sum(identity(rows) * weight_ref[...], axis=1, keepdims=True)
        weight = weight * (1.0 / math.sqrt(pixels))
        eye = identity(128).astype(BF16)
        pad = jnp.zeros((64 - rows, 128), F32)
        found = dot(sky[...], table[:, 256 * h : 256 * (h + 1)], NN)
        for p in range(2):
            wave[p] = found[:, 128 * p : 128 * (p + 1)]
        for c in range(chans):
            real, imag = (wave[p, pl.ds(c, rows, stride=chans), :] * weight for p in range(2))
            both = jnp.concatenate([real, pad, imag, pad], axis=0).astype(BF16)
            wide[pl.ds(c, 128, stride=chans), :] = dot(eye, both, NT)
        for i in range(half):
            turned = wide[NB * chans * i : NB * chans * (i + 1), :].astype(BF16)
            msg[half * h + i] = turned.reshape(NB, chans, 128)
        if h == 0:
            pl.semaphore_wait(barrier, NB + 2)
            exchange(msg, got, 0, ORDER[0])
        else:
            for i in range(1, AHEAD):
                exchange(msg, got, 0, ORDER[i])

    def early_send(_):
        early[y] = msg[EARLY]
        for slot in (0, 1):
            gather_copy(slot, EARLY).start()

    def early_pass(_):
        for slot in (0, 1):
            gather_copy(slot, EARLY).wait_recv()
            gather_copy(3 + slot, EARLY).start()

    def early_exchange(_):
        for slot in (3, 4):
            gather_copy(slot, EARLY).wait_recv()
        exchange(msg, got, 0, EARLY)

    def assemble_early():
        for owner in range(GY):
            at = pl.ds(pl.multiple_of(chans * (2 * owner + core), chans), chans)
            for p in range(2):
                pieces = [late[s, owner, :, 64 * p : 64 * p + rows] for s in range(NB)]
                spec[EARLY, p, at, :] = jnp.concatenate(pieces, axis=1)
        for slot in (2, 5, 6, 7, 8):
            gather_copy(slot, EARLY).start()

    def assemble(i):
        exchanged(msg, got, 0, i).wait_recv()
        own_copy(msg, got, 0, i).wait()
        if i == EARLY:
            assemble_early()
            return
        later = ORDER.index(i) + AHEAD
        if later < modes - 1:
            exchange(msg, got, 0, ORDER[later])
        mine = pl.ds(pl.multiple_of(chans * k, chans), chans)
        for p in range(2):
            pieces = [got[i, s, :, 64 * p : 64 * p + rows] for s in range(NB)]
            spec[i, p, mine, :] = jnp.concatenate(pieces, axis=1)
        for slot in range(3):
            gather_copy(slot, i).start()

    def pass_on(i):
        if i == EARLY:
            return
        for n in range(2):
            gather_copy(n, i).wait_recv()
            gather_copy(3 + n, i).start()
            gather_copy(5 + n, i).start()

    def pass_far(i):
        if i == EARLY:
            return
        for n in range(2):
            gather_copy(3 + n, i).wait_recv()
            gather_copy(7 + n, i).start()

    each = 16 // per
    rounds = bands // each // UNROLL

    def channels(g, _):
        row_group = lax.div(lax.broadcasted_iota(jnp.int32, (16, 128), 0), per)
        for u in range(UNROLL):
            at = pl.multiple_of(16 * (UNROLL * g + u), 16)
            left = coef[pl.ds(at, 16), :].astype(BF16)
            square = kl[pl.ds(each * (UNROLL * g + u), each)]
            mixed = dot(left, square.reshape(each * 128, 128), NT)
            picked = mixed[:, :128]
            for t in range(1, each):
                picked = jnp.where(row_group == t, mixed[:, 128 * t : 128 * (t + 1)], picked)
            filt[pl.ds(at, 16), :] = picked
        return 0

    def analyse(g):
        if g == 0:
            load_leg.wait()
            load_kl.wait()
        degree = k * bands + lax.broadcasted_iota(jnp.int32, (bands, 128), 0)
        for n in range(GROUP):
            i = ORDER[GROUP * g + n]
            for slot in (2, 5, 6, 7, 8):
                gather_copy(slot, i).wait_recv()
            sums = dot(leg[i], spec[i].reshape(2 * 128, cycles), NT)
            for p in range(2):
                kept = jnp.where(degree >= b * modes + i, sums[:, 128 * p : 128 * (p + 1)], 0.0)
                coef[pl.ds(2 * n + p, bands, stride=per), :] = kept
        lax.fori_loop(0, rounds // 2, channels, 0)

    def synthesise(g):
        lax.fori_loop(rounds // 2, rounds, channels, 0)
        for n in range(GROUP):
            i = ORDER[GROUP * g + n]
            sides = [filt[pl.ds(2 * n + p, bands, stride=per), :].astype(BF16) for p in range(2)]
            left = jnp.concatenate(sides, axis=1).T
            for at in range(0, cycles, 256):
                tile = dot(left, leg[i, :, at : at + 256], NN).astype(BF16)
                for p in range(2):
                    for o in range(8):
                        first = 128 * p + 16 * o
                        part[i, o % 2, p, o // 2, :, at : at + 256] = tile[first : first + 16]
            scatter_copy(0, i).start()

    def add_sibling(i):
        scatter_copy(0, i).wait_recv()

        def add(p, _):
            total = part[i, core, p].astype(F32) + sib_part[i, p].astype(F32)
            part[i, core, p] = total.astype(BF16)
            return 0

        lax.fori_loop(0, 2, add, 0)
        for slot in (1, 2, 3, 4):
            scatter_copy(slot, i).start()

    def add_transit(i):
        for n, nearer in ((0, y_up), (1, y_dn)):
            scatter_copy(1 + n, i).wait_recv()
            total = transit[n, i].astype(F32) + part[i, core, n, nearer].astype(F32)
            transit[n, i] = total.astype(BF16)
            scatter_copy(5 + n, i).start()

    def answer(i):
        for slot in (3, 4, 5, 6):
            scatter_copy(slot, i).wait_recv()
        zeros = jnp.zeros((16, 64 - rows), F32)
        both = [
            part[i, core, p, y].astype(F32)
            + from_up[p, i].astype(F32)
            + from_dn[p, i].astype(F32)
            for p in range(2)
        ]
        for s in range(NB):
            lanes = slice(rows * s, rows * (s + 1))
            line = jnp.concatenate([both[0][:, lanes], zeros, both[1][:, lanes], zeros], axis=1)
            reply[i, s] = line.astype(BF16)
        exchange(reply, back, 1, i)

    def finish(h):
        eye = identity(128).astype(BF16)
        for i in range(half):
            exchanged(reply, back, 1, half * h + i).wait_recv()
            own_copy(reply, back, 1, half * h + i).wait()
            turned = back[half * h + i].reshape(NB * chans, 128)
            wide[NB * chans * i : NB * chans * (i + 1), :] = turned.astype(F32)
        for c in range(chans):
            here = wide[pl.ds(c, 128, stride=chans), :].astype(BF16)
            turned = dot(eye, here, NT)
            for p in range(2):
                wave[p, pl.ds(c, rows, stride=chans), :] = turned[64 * p : 64 * p + rows]
        for p in range(2):
            at = 256 * h + 128 * p
            out_ref[:, at : at + 128] = wave[p].astype(BF16)

    stages = {
        f.__name__: f
        for f in (
            transform,
            early_send,
            early_pass,
            early_exchange,
            assemble,
            pass_on,
            pass_far,
            analyse,
            synthesise,
            add_sibling,
            add_transit,
            answer,
            finish,
        )
    }
    for name, i in plan():
        by_mode = name in ("assemble", "pass_on", "pass_far", "add_sibling", "add_transit", "answer")
        stages[name](ORDER[i] if by_mode else i)

    for i in range(modes):
        exchanged(msg, got, 0, i).wait_send()
        exchanged(reply, back, 1, i).wait_send()
        for slot in range(9):
            gather_copy(slot, i).wait_send()
        for slot in range(7):
            scatter_copy(slot, i).wait_send()


def main_call(sky, weight, table, legendre, kl):
    modes, bands, cycles = legendre.shape
    chans, (lines, pixels) = 16, sky.shape
    per = 2 * GROUP
    vmem = pl.BlockSpec(memory_space=pltpu.VMEM)
    hbm = pl.BlockSpec(memory_space=pl.ANY)
    dma = pltpu.SemaphoreType.DMA
    messages = pltpu.VMEM((modes, NB, chans, 128), BF16)
    return pl.pallas_call(
        main_kernel,
        out_shape=jax.ShapeDtypeStruct((lines, 512), BF16),
        in_specs=[hbm, vmem, hbm, hbm, hbm],
        out_specs=vmem,
        scratch_shapes=[
            pltpu.VMEM(sky.shape, BF16),
            pltpu.VMEM(table.shape, BF16),
            pltpu.VMEM(legendre.shape, BF16),
            pltpu.VMEM(kl.shape, BF16),
            pltpu.VMEM((2, lines, 128), F32),
            pltpu.VMEM((modes // 2 * NB * chans, 128), F32),
            messages,
            messages,
            pltpu.VMEM((GY, NB, chans, 128), BF16),
            pltpu.VMEM((NB, GY, chans, 128), BF16),
            pltpu.VMEM((modes, 2, 128, cycles), BF16),
            pltpu.VMEM((bands * per, 128), F32),
            pltpu.VMEM((bands * per, 128), F32),
            pltpu.VMEM((modes, 2, 2, GY, chans, cycles), BF16),
            pltpu.VMEM((modes, 2, GY, chans, cycles), BF16),
            pltpu.VMEM((2, modes, chans, cycles), BF16),
            pltpu.VMEM((2, modes, chans, cycles), BF16),
            pltpu.VMEM((2, modes, chans, cycles), BF16),
            messages,
            messages,
            dma((4,)),
            dma((2, modes)),
            dma((2, 2, modes)),
            dma((modes, 9)),
            dma((modes, 9)),
            dma((modes, 7)),
            dma((modes, 7)),
        ],
        compiler_params=pltpu.CompilerParams(
            collective_id=0, has_side_effects=True, vmem_limit_bytes=VMEM_LIMIT
        ),
        cost_estimate=pl.CostEstimate(
            flops=8 * 10**9, bytes_accessed=18 * 10**6, transcendentals=0
        ),
    )(sky, weight, table, legendre, kl)


def inverse_kernel(scale, field_ref, table_ref, out_ref):
    out_ref[...] = (dot(field_ref[...], table_ref[...], NN) * scale).astype(BF16)


def inverse(field, table):
    lines, pixels = field.shape[0], table.shape[1]
    block = BLOCK
    return pl.pallas_call(
        functools.partial(inverse_kernel, 1.0 / math.sqrt(pixels)),
        grid=(pixels // block,),
        out_shape=jax.ShapeDtypeStruct((lines, pixels), BF16),
        in_specs=[
            pl.BlockSpec(field.shape, lambda i: (0, 0)),
            pl.BlockSpec((512, block), lambda i: (0, i)),
        ],
        out_specs=pl.BlockSpec((lines, block), lambda i: (0, i)),
        compiler_params=pltpu.CompilerParams(vmem_limit_bytes=VMEM_LIMIT),
    )(field, table)


def shards(sky_map, cycle_weight, legendre, kl_filter):
    rows, chans, pixels = sky_map.shape
    table = fourier_table(pixels, legendre.shape[0] * NB)
    sky = sky_map.reshape(rows * chans, pixels)
    weight = cycle_weight.reshape(1, rows)
    field = main_call(sky, weight, jnp.asarray(table), legendre, kl_filter)
    return inverse(field, jnp.asarray(table.T.copy())).reshape(rows, chans, pixels)


def solution(mesh):
    in_specs = (P("blk", "chan", None), P("blk"), P("blk", "chan", None), P("chan", None, None))
    out_specs = P("blk", "chan", None)
    return jax.shard_map(shards, mesh=mesh, in_specs=in_specs, out_specs=out_specs, check_vma=False)
```

```python
import functools
import math

import jax
import jax.numpy as jnp
import numpy as np
from jax import lax
from jax.experimental import pallas as pl
from jax.experimental.pallas import tpu as pltpu
from jax.sharding import PartitionSpec as P

F32, BF16 = jnp.float32, jnp.bfloat16
MESH = pl.DeviceIdType.MESH
NT = (((1,), (1,)), ((), ()))
NN = (((1,), (0,)), ((), ()))
VMEM_LIMIT = 60 * 2**20
GX, GZ, GY = 4, 8, 4
NB = GX * GZ
MODES, GROUP = 8, 2
UNROLL = 24
BLOCK = 1024
AHEAD = 3
SCATTER, WINDOW, LAG = 3, 1, 2
ORDER = (0, 1, 2, 4, 5, 6, 7, 3)
EARLY = ORDER[-1]


def fourier_table(pixel_count, mode_count):
    phase = np.arange(pixel_count)[:, None] * np.arange(mode_count)[None, :] % pixel_count
    angles = phase.astype(np.float32) * np.float32(2.0 * math.pi / pixel_count)
    both = np.stack([np.cos(angles), -np.sin(angles)], axis=1).astype(jnp.bfloat16)
    both = both.reshape(pixel_count, 2, NB, 2, MODES // 2)
    return both.transpose(0, 3, 1, 4, 2).reshape(pixel_count, 2 * mode_count)


def identity(size):
    rows = lax.broadcasted_iota(jnp.int32, (size, size), 0)
    cols = lax.broadcasted_iota(jnp.int32, (size, size), 1)
    return jnp.where(rows == cols, 1.0, 0.0)


def dot(a, b, dims):
    return lax.dot_general(a, b, dims, preferred_element_type=F32)


def plan():
    steps = [("transform", 0), ("early_send", 0), ("transform", 1), ("early_pass", 0)]
    steps += [("assemble", 0), ("assemble", 1), ("pass_on", 0)]
    for t in range(MODES + SCATTER + 4):
        steps += [("early_exchange", t - 3)]
        steps += [("assemble", t + 2 if t + 2 < MODES - 1 else -1)]
        steps += [("pass_on", t + 1), ("pass_far", t)]
        r = t - SCATTER
        steps += [("add_transit", r - 1)]
        steps += [("add_sibling", i) for i in range(WINDOW - 1) if r == 0]
        steps += [("add_sibling", r + WINDOW - 1 if r >= 0 else -1), ("answer", r - LAG)]
        steps += [("assemble", MODES - 1 if t == MODES - 1 else -1)]
        if t % 2:
            steps += [("analyse", (t - 1) // 2)]
        else:
            steps += [("synthesise", (t - 2) // 2)]
    steps += [("finish", 1), ("finish", 0)]
    count = {"transform": 2, "finish": 2, "analyse": MODES // GROUP, "synthesise": MODES // GROUP}
    count |= {"early_send": 1, "early_pass": 1, "early_exchange": 1}
    return [(name, i) for name, i in steps if 0 <= i < count.get(name, MODES)]


def main_kernel(
    sky_hbm,
    weight_ref,
    table_hbm,
    leg_hbm,
    kl_hbm,
    out_ref,
    sky,
    table,
    leg,
    kl,
    wave,
    wide,
    msg,
    got,
    early,
    late,
    spec,
    coef,
    filt,
    part,
    sib_part,
    transit,
    from_up,
    from_dn,
    reply,
    back,
    load_sem,
    own_sem,
    a2a_sem,
    ag_send,
    ag_recv,
    rs_send,
    rs_recv,
):
    modes, bands, cycles = leg.shape
    chans, pixels = 16, sky.shape[1]
    rows = sky.shape[0] // chans
    half = modes // 2
    per = 2 * GROUP
    b = lax.axis_index("blk")
    k = lax.axis_index("chan")
    y, core = lax.div(k, 2), lax.rem(k, 2)
    y_up, y_dn, y_far = lax.rem(y + 1, GY), lax.rem(y + GY - 1, GY), lax.rem(y + 2, GY)
    up, dn, far, sib = 2 * y_up + core, 2 * y_dn + core, 2 * y_far + core, 2 * y + 1 - core

    load_sky = pltpu.make_async_copy(sky_hbm, sky, load_sem.at[0])
    load_table = pltpu.make_async_copy(table_hbm, table, load_sem.at[1])
    load_leg = pltpu.make_async_copy(leg_hbm, leg, load_sem.at[2])
    load_kl = pltpu.make_async_copy(kl_hbm, kl, load_sem.at[3])
    load_sky.start()
    load_table.start()

    barrier = pltpu.get_barrier_semaphore()
    for other in (up, dn, sib):
        pl.semaphore_signal(barrier, inc=1, device_id={"chan": other}, device_id_type=MESH)

    def greet(j, _):
        pl.semaphore_signal(
            barrier, inc=1, device_id={"blk": lax.rem(b + j, NB)}, device_id_type=MESH
        )
        return 0

    lax.fori_loop(1, NB, greet, 0)

    def own_copy(src, dst, which, i):
        if which == 0 and i == EARLY:
            return pltpu.make_async_copy(early.at[:, b], late.at[b], own_sem.at[which, i])
        return pltpu.make_async_copy(src.at[i, b], dst.at[i, b], own_sem.at[which, i])

    def exchange(src, dst, which, i):
        def send(j):
            to = lax.rem(b + j, NB)
            first = which == 0 and i == EARLY
            pltpu.make_async_remote_copy(
                src_ref=early.at[:, to] if first else src.at[i, to],
                dst_ref=late.at[b] if first else dst.at[i, b],
                send_sem=a2a_sem.at[which, 0, i],
                recv_sem=a2a_sem.at[which, 1, i],
                device_id={"blk": to},
                device_id_type=MESH,
            ).start()

        def pair(j, _):
            send(j)
            send(NB - j)
            return 0

        lax.fori_loop(1, NB // 2, pair, 0)
        send(NB // 2)
        own_copy(src, dst, which, i).start()

    def exchanged(src, dst, which, i):
        some = pl.ds(0, NB - 1)
        first = which == 0 and i == EARLY
        return pltpu.make_async_remote_copy(
            src_ref=late.at[some] if first else src.at[i, some],
            dst_ref=late.at[some] if first else dst.at[i, some],
            send_sem=a2a_sem.at[which, 0, i],
            recv_sem=a2a_sem.at[which, 1, i],
            device_id={"chan": sib},
            device_id_type=MESH,
        )

    def copy(src, dst, send, recv, slot, i, to):
        return pltpu.make_async_remote_copy(
            src_ref=src,
            dst_ref=dst,
            send_sem=send.at[i, slot],
            recv_sem=recv.at[i, slot],
            device_id={"chan": to},
            device_id_type=MESH,
        )

    def shard(i, owner, p=None):
        at = pl.ds(pl.multiple_of(chans * owner, chans), chans)
        return spec.at[i, :, at, :] if p is None else spec.at[i, p, at, :]

    def gather_copy(slot, i):
        src, to = (
            (shard(i, k), up),
            (shard(i, k), dn),
            (shard(i, k), sib),
            (shard(i, dn, 0), up),
            (shard(i, up, 1), dn),
            (shard(i, dn), sib),
            (shard(i, up), sib),
            (shard(i, far, 0), sib),
            (shard(i, far, 1), sib),
        )[slot]
        if i == EARLY and slot in (0, 1, 3, 4):
            src = (
                early.at[y],
                early.at[y],
                None,
                early.at[y_dn, pl.ds(0, NB // 2)],
                early.at[y_up, pl.ds(NB // 2, NB // 2)],
            )[slot]
        return copy(src, src, ag_send, ag_recv, slot, i, to)

    def scatter_copy(slot, i):
        src, dst, to = (
            (part.at[i, 1 - core], sib_part.at[i], sib),
            (part.at[i, core, 0, y_far], transit.at[0, i], up),
            (part.at[i, core, 1, y_far], transit.at[1, i], dn),
            (part.at[i, core, 1, y_up], from_dn.at[1, i], up),
            (part.at[i, core, 0, y_dn], from_up.at[0, i], dn),
            (transit.at[0, i], from_dn.at[0, i], up),
            (transit.at[1, i], from_up.at[1, i], dn),
        )[slot]
        return copy(src, dst, rs_send, rs_recv, slot, i, to)

    def transform(h):
        if h == 0:
            load_sky.wait()
            load_table.wait()
            load_leg.start()
            load_kl.start()
        weight = jnp.sum(identity(rows) * weight_ref[...], axis=1, keepdims=True)
        weight = weight * (1.0 / math.sqrt(pixels))
        eye = identity(128).astype(BF16)
        pad = jnp.zeros((64 - rows, 128), F32)
        found = dot(sky[...], table[:, 256 * h : 256 * (h + 1)], NN)
        for p in range(2):
            wave[p] = found[:, 128 * p : 128 * (p + 1)]
        for c in range(chans):
            real, imag = (wave[p, pl.ds(c, rows, stride=chans), :] * weight for p in range(2))
            both = jnp.concatenate([real, pad, imag, pad], axis=0).astype(BF16)
            wide[pl.ds(c, 128, stride=chans), :] = dot(eye, both, NT)
        for i in range(half):
            turned = wide[NB * chans * i : NB * chans * (i + 1), :].astype(BF16)
            msg[half * h + i] = turned.reshape(NB, chans, 128)
        if h == 0:
            pl.semaphore_wait(barrier, NB + 2)
            exchange(msg, got, 0, ORDER[0])
        else:
            for i in range(1, AHEAD):
                exchange(msg, got, 0, ORDER[i])

    def early_send(_):
        early[y] = msg[EARLY]
        for slot in (0, 1):
            gather_copy(slot, EARLY).start()

    def early_pass(_):
        for slot in (0, 1):
            gather_copy(slot, EARLY).wait_recv()
            gather_copy(3 + slot, EARLY).start()

    def early_exchange(_):
        for slot in (3, 4):
            gather_copy(slot, EARLY).wait_recv()
        exchange(msg, got, 0, EARLY)

    def assemble_early():
        for owner in range(GY):
            at = pl.ds(pl.multiple_of(chans * (2 * owner + core), chans), chans)
            for p in range(2):
                pieces = [late[s, owner, :, 64 * p : 64 * p + rows] for s in range(NB)]
                spec[EARLY, p, at, :] = jnp.concatenate(pieces, axis=1)
        for slot in (2, 5, 6, 7, 8):
            gather_copy(slot, EARLY).start()

    def assemble(i):
        exchanged(msg, got, 0, i).wait_recv()
        own_copy(msg, got, 0, i).wait()
        if i == EARLY:
            assemble_early()
            return
        later = ORDER.index(i) + AHEAD
        if later < modes - 1:
            exchange(msg, got, 0, ORDER[later])
        mine = pl.ds(pl.multiple_of(chans * k, chans), chans)
        for p in range(2):
            pieces = [got[i, s, :, 64 * p : 64 * p + rows] for s in range(NB)]
            spec[i, p, mine, :] = jnp.concatenate(pieces, axis=1)
        for slot in range(3):
            gather_copy(slot, i).start()

    def pass_on(i):
        if i == EARLY:
            return
        for n in range(2):
            gather_copy(n, i).wait_recv()
            gather_copy(3 + n, i).start()
            gather_copy(5 + n, i).start()

    def pass_far(i):
        if i == EARLY:
            return
        for n in range(2):
            gather_copy(3 + n, i).wait_recv()
            gather_copy(7 + n, i).start()

    each = 16 // per
    rounds = bands // each // UNROLL

    def channels(g, _):
        row_group = lax.div(lax.broadcasted_iota(jnp.int32, (16, 128), 0), per)
        for u in range(UNROLL):
            at = pl.multiple_of(16 * (UNROLL * g + u), 16)
            left = coef[pl.ds(at, 16), :].astype(BF16)
            square = kl[pl.ds(each * (UNROLL * g + u), each)]
            mixed = dot(left, square.reshape(each * 128, 128), NT)
            picked = mixed[:, :128]
            for t in range(1, each):
                picked = jnp.where(row_group == t, mixed[:, 128 * t : 128 * (t + 1)], picked)
            filt[pl.ds(at, 16), :] = picked
        return 0

    def analyse(g):
        if g == 0:
            load_leg.wait()
            load_kl.wait()
        degree = k * bands + lax.broadcasted_iota(jnp.int32, (bands, 128), 0)
        for n in range(GROUP):
            i = ORDER[GROUP * g + n]
            for slot in (2, 5, 6, 7, 8):
                gather_copy(slot, i).wait_recv()
            sums = dot(leg[i], spec[i].reshape(2 * 128, cycles), NT)
            for p in range(2):
                kept = jnp.where(degree >= b * modes + i, sums[:, 128 * p : 128 * (p + 1)], 0.0)
                coef[pl.ds(2 * n + p, bands, stride=per), :] = kept
        lax.fori_loop(0, rounds // 2, channels, 0)

    def synthesise(g):
        lax.fori_loop(rounds // 2, rounds, channels, 0)
        for n in range(GROUP):
            i = ORDER[GROUP * g + n]
            sides = [filt[pl.ds(2 * n + p, bands, stride=per), :].astype(BF16) for p in range(2)]
            left = jnp.concatenate(sides, axis=1).T
            for at in range(0, cycles, 256):
                tile = dot(left, leg[i, :, at : at + 256], NN).astype(BF16)
                for p in range(2):
                    for o in range(8):
                        first = 128 * p + 16 * o
                        part[i, o % 2, p, o // 2, :, at : at + 256] = tile[first : first + 16]
            scatter_copy(0, i).start()

    def add_sibling(i):
        scatter_copy(0, i).wait_recv()

        def add(p, _):
            total = part[i, core, p].astype(F32) + sib_part[i, p].astype(F32)
            part[i, core, p] = total.astype(BF16)
            return 0

        lax.fori_loop(0, 2, add, 0)
        for slot in (1, 2, 3, 4):
            scatter_copy(slot, i).start()

    def add_transit(i):
        for n, nearer in ((0, y_up), (1, y_dn)):
            scatter_copy(1 + n, i).wait_recv()
            total = transit[n, i].astype(F32) + part[i, core, n, nearer].astype(F32)
            transit[n, i] = total.astype(BF16)
            scatter_copy(5 + n, i).start()

    def answer(i):
        for slot in (3, 4, 5, 6):
            scatter_copy(slot, i).wait_recv()
        zeros = jnp.zeros((16, 64 - rows), F32)
        both = [
            part[i, core, p, y].astype(F32)
            + from_up[p, i].astype(F32)
            + from_dn[p, i].astype(F32)
            for p in range(2)
        ]
        for s in range(NB):
            lanes = slice(rows * s, rows * (s + 1))
            line = jnp.concatenate([both[0][:, lanes], zeros, both[1][:, lanes], zeros], axis=1)
            reply[i, s] = line.astype(BF16)
        exchange(reply, back, 1, i)

    def finish(h):
        eye = identity(128).astype(BF16)
        for i in range(half):
            exchanged(reply, back, 1, half * h + i).wait_recv()
            own_copy(reply, back, 1, half * h + i).wait()
            turned = back[half * h + i].reshape(NB * chans, 128)
            wide[NB * chans * i : NB * chans * (i + 1), :] = turned.astype(F32)
        for c in range(chans):
            here = wide[pl.ds(c, 128, stride=chans), :].astype(BF16)
            turned = dot(eye, here, NT)
            for p in range(2):
                wave[p, pl.ds(c, rows, stride=chans), :] = turned[64 * p : 64 * p + rows]
        for p in range(2):
            at = 256 * h + 128 * p
            out_ref[:, at : at + 128] = wave[p].astype(BF16)

    stages = {
        f.__name__: f
        for f in (
            transform,
            early_send,
            early_pass,
            early_exchange,
            assemble,
            pass_on,
            pass_far,
            analyse,
            synthesise,
            add_sibling,
            add_transit,
            answer,
            finish,
        )
    }
    for name, i in plan():
        by_mode = name in ("assemble", "pass_on", "pass_far", "add_sibling", "add_transit", "answer")
        stages[name](ORDER[i] if by_mode else i)

    for i in range(modes):
        exchanged(msg, got, 0, i).wait_send()
        exchanged(reply, back, 1, i).wait_send()
        for slot in range(9):
            gather_copy(slot, i).wait_send()
        for slot in range(7):
            scatter_copy(slot, i).wait_send()


def main_call(sky, weight, table, legendre, kl):
    modes, bands, cycles = legendre.shape
    chans, (lines, pixels) = 16, sky.shape
    per = 2 * GROUP
    vmem = pl.BlockSpec(memory_space=pltpu.VMEM)
    hbm = pl.BlockSpec(memory_space=pl.ANY)
    dma = pltpu.SemaphoreType.DMA
    messages = pltpu.VMEM((modes, NB, chans, 128), BF16)
    return pl.pallas_call(
        main_kernel,
        out_shape=jax.ShapeDtypeStruct((lines, 512), BF16),
        in_specs=[hbm, vmem, hbm, hbm, hbm],
        out_specs=vmem,
        scratch_shapes=[
            pltpu.VMEM(sky.shape, BF16),
            pltpu.VMEM(table.shape, BF16),
            pltpu.VMEM(legendre.shape, BF16),
            pltpu.VMEM(kl.shape, BF16),
            pltpu.VMEM((2, lines, 128), F32),
            pltpu.VMEM((modes // 2 * NB * chans, 128), F32),
            messages,
            messages,
            pltpu.VMEM((GY, NB, chans, 128), BF16),
            pltpu.VMEM((NB, GY, chans, 128), BF16),
            pltpu.VMEM((modes, 2, 128, cycles), BF16),
            pltpu.VMEM((bands * per, 128), F32),
            pltpu.VMEM((bands * per, 128), F32),
            pltpu.VMEM((modes, 2, 2, GY, chans, cycles), BF16),
            pltpu.VMEM((modes, 2, GY, chans, cycles), BF16),
            pltpu.VMEM((2, modes, chans, cycles), BF16),
            pltpu.VMEM((2, modes, chans, cycles), BF16),
            pltpu.VMEM((2, modes, chans, cycles), BF16),
            messages,
            messages,
            dma((4,)),
            dma((2, modes)),
            dma((2, 2, modes)),
            dma((modes, 9)),
            dma((modes, 9)),
            dma((modes, 7)),
            dma((modes, 7)),
        ],
        compiler_params=pltpu.CompilerParams(
            collective_id=0, has_side_effects=True, vmem_limit_bytes=VMEM_LIMIT
        ),
        cost_estimate=pl.CostEstimate(
            flops=8 * 10**9, bytes_accessed=18 * 10**6, transcendentals=0
        ),
    )(sky, weight, table, legendre, kl)


def inverse_kernel(scale, field_ref, table_ref, out_ref):
    out_ref[...] = (dot(field_ref[...], table_ref[...], NN) * scale).astype(BF16)


def inverse(field, table):
    lines, pixels = field.shape[0], table.shape[1]
    block = BLOCK
    return pl.pallas_call(
        functools.partial(inverse_kernel, 1.0 / math.sqrt(pixels)),
        grid=(pixels // block,),
        out_shape=jax.ShapeDtypeStruct((lines, pixels), BF16),
        in_specs=[
            pl.BlockSpec(field.shape, lambda i: (0, 0)),
            pl.BlockSpec((512, block), lambda i: (0, i)),
        ],
        out_specs=pl.BlockSpec((lines, block), lambda i: (0, i)),
        compiler_params=pltpu.CompilerParams(vmem_limit_bytes=VMEM_LIMIT),
    )(field, table)


def shards(sky_map, cycle_weight, legendre, kl_filter):
    rows, chans, pixels = sky_map.shape
    table = fourier_table(pixels, legendre.shape[0] * NB)
    sky = sky_map.reshape(rows * chans, pixels)
    weight = cycle_weight.reshape(1, rows)
    field = main_call(sky, weight, jnp.asarray(table), legendre, kl_filter)
    return inverse(field, jnp.asarray(table.T.copy())).reshape(rows, chans, pixels)


def solution(mesh):
    in_specs = (P("blk", "chan", None), P("blk"), P("blk", "chan", None), P("chan", None, None))
    out_specs = P("blk", "chan", None)
    return jax.shard_map(shards, mesh=mesh, in_specs=in_specs, out_specs=out_specs, check_vma=False)
```
